32 devices in a mesh: seq: 4 (over z), dp: 8 (over y, x, core).
Axes of the slice: x: 2, y: 2, z: 4, core: 2. Of those that a mesh axis runs over, the one named last changes fastest.
Arguments:
- block_input: float32 [192, 1024, 768], P('dp', 'seq'), may hold values from -800 to 800
- first_gain: float32 [768], replicated, may hold values from 0.1 to 1.9
- first_shift: float32 [768], replicated, may hold values from -3 to 3
- dilated_weight: float32 [3, 768, 384], replicated, may hold values from -0.125 to 0.125
- second_gain: float32 [384], replicated, may hold values from 0.1 to 1.9
- second_shift: float32 [384], replicated, may hold values from -3 to 3
- point_weight: float32 [384, 768], replicated, may hold values from -0.3125 to 0.3125
- cotangent: float32 [192, 1024, 768], P('dp', 'seq'), may hold values from -6 to 6
Outputs:
- block_output: float32 [192, 1024, 768], P('dp', 'seq')
- input_grad: float32 [192, 1024, 768], P('dp', 'seq')
- first_gain_grad: float32 [768], replicated
- first_shift_grad: float32 [768], replicated
- dilated_grad: float32 [3, 768, 384], replicated
- second_gain_grad: float32 [384], replicated
- second_shift_grad: float32 [384], replicated
- point_grad: float32 [384, 768], replicated
The draws below stay inside these ranges and needn't reach their ends.
All inputs are finite; a program needn't handle non-finite values.
Results may differ from the reference program's by a relative error of at most 0.0003.
Values sent between devices are 32-bit elements; how exact they have to be, the bound alone decides.
No kernel may reach another device: no remote copies, remote signals or barrier semaphores. Data moves between devices by JAX's collectives and lax.ppermute only.
A program may use at most 256 MiB of HBM per device.

```python
import jax
import jax.numpy as jnp
from jax import lax

C = 768
MID = 384
DILATION_STEP = 57
BINS = 1024
WINDOWS = 192


def draw_block_input(key, part):
    key = jax.random.fold_in(key, 11)
    subkeys = jax.random.split(key, 4)
    channel_scale = jnp.exp(jax.random.uniform(subkeys[0], (C,), jnp.float32, 0.0, 2.302585))
    channel_center = jnp.clip(jax.random.normal(subkeys[1], (C,), jnp.float32), -4.0, 4.0) * channel_scale * 0.8
    window_rise = 3.0 ** (jnp.arange(WINDOWS, dtype=jnp.float32) / max(WINDOWS - 1, 1))
    window_rise = window_rise * jax.random.uniform(subkeys[2], (WINDOWS,), jnp.float32, 0.8, 1.2)
    bin_rise = 2.0 ** (jnp.arange(BINS, dtype=jnp.float32) / max(BINS - 1, 1))
    random_part = jnp.clip(jax.random.normal(subkeys[3], (WINDOWS, BINS, C), jnp.float32), -5.0, 5.0)
    feature_values = channel_center + channel_scale * random_part
    return (feature_values * window_rise[:, None, None] * bin_rise[None, :, None]).astype(jnp.float32)


def block_levels(own_key, shape, cuts, smallest, high):
    level = 1.0
    for position, shards_of in cuts:
        heights = jax.random.uniform(jax.random.fold_in(jax.random.fold_in(own_key, 6), position), (shards_of,), jnp.float32, smallest / len(cuts), high / len(cuts))
        level = level * jnp.repeat(jnp.exp(heights), shape[position] // shards_of).reshape((-1,) + (1,) * (len(shape) - 1 - position))
    return level


def scatter_about(own_key, extent, scale, bound, cuts=(), kind=jnp.bfloat16):
    values = scale * jax.random.normal(own_key, extent, jnp.float32)
    if cuts:
        values = values * block_levels(own_key, extent, cuts, -0.22, 0.18)
    return jnp.clip(values, -bound, bound).astype(kind)


def setup_inputs(seed: int = 0) -> dict:
    key_of = jax.random.split(jax.random.key(seed), 9)
    return {
        "block_input": draw_block_input(jax.random.fold_in(key_of[8], 71), 0),
        "first_gain": jnp.clip(1.0 + 0.18 * jax.random.normal(key_of[1], (C,), jnp.float32), 0.1, 1.9),
        "first_shift": scatter_about(key_of[2], (C,), 0.5, 3.0, (), jnp.float32),
        "dilated_weight": scatter_about(key_of[3], (3, C, MID), (3 * C) ** -0.5, 0.125, (), jnp.float32),
        "second_gain": jnp.clip(1.0 + 0.18 * jax.random.normal(key_of[4], (MID,), jnp.float32), 0.1, 1.9),
        "second_shift": scatter_about(key_of[5], (MID,), 0.5, 3.0, (), jnp.float32),
        "point_weight": scatter_about(key_of[6], (MID, C), MID ** -0.5, 0.3125, (), jnp.float32),
        "cotangent": scatter_about(key_of[7], (WINDOWS, BINS, C), 1.0, 6.0, ((0, 8), (1, 4)), jnp.float32),
    }


EPS = 1e-05

def normalize(feature_values, gain, shift):
    center = lax.optimization_barrier(jnp.mean(feature_values, axis=(0, 1)))
    offset = feature_values - center
    spread = lax.optimization_barrier(jnp.mean(offset * offset, axis=(0, 1)))
    return gain * (offset * lax.rsqrt(spread + EPS)) + shift

def dilated(feature_values, kernel_weight):
    padded_input = jnp.pad(feature_values, ((0, 0), (DILATION_STEP, DILATION_STEP), (0, 0)))
    total = jnp.zeros((feature_values.shape[0], feature_values.shape[1], kernel_weight.shape[2]), jnp.float32)
    for kernel_tap_index in range(3):
        window_slice = padded_input[:, kernel_tap_index * DILATION_STEP:kernel_tap_index * DILATION_STEP + feature_values.shape[1]]
        total = total + jnp.einsum('oxi,ik->oxk', window_slice, kernel_weight[kernel_tap_index], precision=lax.Precision.HIGHEST)
    return total

def forward(block_input, first_gain, first_shift, dilated_weight, second_gain, second_shift, point_weight):
    first_activation = jax.nn.gelu(normalize(block_input, first_gain, first_shift), approximate=False)
    middle_features = dilated(first_activation, dilated_weight)
    act_second = jax.nn.gelu(normalize(middle_features, second_gain, second_shift), approximate=False)
    branch = jnp.einsum('wbm,mc->wbc', act_second, point_weight, precision=lax.Precision.HIGHEST)
    return block_input + branch

def reference(block_input, first_gain, first_shift, dilated_weight, second_gain, second_shift, point_weight, cotangent):
    result, pullback = jax.vjp(forward, block_input, first_gain, first_shift, dilated_weight, second_gain, second_shift, point_weight)
    grads = pullback(cotangent)
    return (result, grads[0], grads[1], grads[2], grads[3], grads[4], grads[5], grads[6])
```

```python
import functools

import jax
import jax.numpy as jnp
from jax import lax
from jax.experimental import pallas as pl
from jax.experimental.pallas import tpu as pltpu
from jax.sharding import Mesh
from jax.sharding import PartitionSpec as P

STEP = 57
EDGE = 64
EPS = 1e-05
LOG2_INV_ROOT_TWO_PI = -1.3257480647361592
HALF_LOG2_E = 0.7213475204444817
MIB = 1024 * 1024
F32 = jnp.float32
BF16 = jnp.bfloat16
DP = ("chip", "core")

PHI = (
    0.7978849414599987,
    0.03633308457510501,
    -3.2594975844072696e-05,
    -5.530619400541097e-05,
    3.964744542062183e-06,
    -1.3226335479189098e-07,
    1.7561713084457843e-09,
)


def gelu_parts(v):
    square = v * v
    poly = PHI[6]
    for k in (5, 4, 3, 2, 1, 0):
        poly = poly * square + PHI[k]
    cdf = 0.5 * jnp.tanh(v * poly) + 0.5
    return v * cdf, cdf + v * jnp.exp2(square * (-HALF_LOG2_E) + LOG2_INV_ROOT_TWO_PI)


def split(v):
    high = v.astype(BF16)
    return high, (v - high.astype(F32)).astype(BF16)


def fold(x):
    return jnp.sum(x, axis=0, keepdims=True)


def dot(left, right):
    return lax.dot_general(left, right, (((1,), (0,)), ((), ())), preferred_element_type=F32)


def dot_rows(left, right):
    return lax.dot_general(left, right, (((0,), (0,)), ((), ())), preferred_element_type=F32)


def call(kernel, grid, ins, outs, scratch=(), vmem=60, flops=0, moved=0, into=(), after=(), into_first=0):
    hold = list(after) + list(into)
    aliases = {len(ins) + len(after) + k: k + into_first for k in range(len(into))}

    def body(*refs):
        kernel(*refs[: len(ins)], *refs[len(ins) + len(hold) :])

    def spec(shape, block, index, keep):
        if block is None:
            return pl.BlockSpec(shape, lambda *i: (0,) * len(shape), pipeline_mode=pl.Buffered(1) if keep else None)
        return pl.BlockSpec(block, index)

    return pl.pallas_call(
        body,
        grid=grid,
        in_specs=[spec(a.shape, b, i, True) for a, b, i in ins] + [pl.BlockSpec(memory_space=pltpu.HBM)] * len(hold),
        out_specs=[spec(s, b, i, False) for s, _, b, i in outs],
        out_shape=[jax.ShapeDtypeStruct(s, d) for s, d, _, _ in outs],
        scratch_shapes=list(scratch),
        compiler_params=pltpu.CompilerParams(vmem_limit_bytes=vmem * MIB),
        input_output_aliases=aliases,
        cost_estimate=pl.CostEstimate(flops=int(flops), bytes_accessed=int(moved), transcendentals=0),
    )(*[a for a, _, _ in ins], *hold)


def add_moments(out_ref, blocks, ref, fresh):
    windows, bins, channels = ref.shape
    rows = windows * bins

    total = eighths(ref[0])
    for w in range(1, windows):
        total = total + eighths(ref[w])
    mean = fold(total) * (1.0 / rows)
    square = None
    for w in range(windows):
        off = ref[w] - mean
        square = eighths(off * off) if square is None else square + eighths(off * off)
    square = fold(square)

    @pl.when(fresh)
    def _():
        out_ref[0:1, :] = mean
        out_ref[1:2, :] = square

    @pl.when(jnp.logical_not(fresh))
    def _():
        n = lax.convert_element_type(blocks, F32)
        share = 1.0 / (n + 1.0)
        delta = mean - out_ref[0:1, :]
        out_ref[0:1, :] = out_ref[0:1, :] + delta * share
        out_ref[1:2, :] = out_ref[1:2, :] + square + delta * delta * (rows * n * share)


def merge_moments(parts, count):
    mean = parts[0][0:1, :]
    for p in parts[1:]:
        mean = mean + p[0:1, :]
    mean = mean * (1.0 / len(parts))
    square = jnp.zeros_like(mean)
    for p in parts:
        off = p[0:1, :] - mean
        square = square + (p[1:2, :] + (off * off) * count)
    return mean, square


def merge_moments_kernel(count, *refs):
    *parts, out_ref = refs
    mean, square = merge_moments(parts, count)
    out_ref[0:1, :] = mean
    out_ref[1:2, :] = square


def peers(array, axis):
    count = lax.axis_size(axis)
    return [array] + [
        lax.ppermute(array, axis, [(i, (i + by) % count) for i in range(count)]) for by in range(1, count)
    ]


def gather_moments(moments, count):
    merged = call(
        functools.partial(merge_moments_kernel, float(count)),
        (),
        [(p, None, None) for p in peers(moments, DP)],
        [(moments.shape, F32, None, None)],
    )[0]
    return peers(merged, "seq")


def gather_sums(sums):
    return peers(functools.reduce(jnp.add, peers(sums, DP)), "seq")


def first_moments_kernel(x_ref, out_ref):
    step = pl.program_id(0)
    add_moments(out_ref, step, x_ref, step == 0)


def as_row(ref):
    return ref[...].reshape(1, ref.shape[0])


def first_finish_kernel(count, total, *refs):
    *parts, gain_ref, shift_ref, par_ref = refs
    mean, square = merge_moments(parts, count)
    inverse = lax.rsqrt(square * (1.0 / total) + EPS)
    par_ref[0:1, :] = mean
    par_ref[1:2, :] = as_row(gain_ref) * inverse
    par_ref[2:3, :] = as_row(shift_ref)
    par_ref[3:4, :] = inverse


def second_finish_kernel(count, total, *refs):
    *parts, gain_ref, shift_ref, par_ref = refs
    mean, square = merge_moments(parts, count)
    par_ref[0:1, :] = mean
    par_ref[1:2, :] = lax.rsqrt(square * (1.0 / total) + EPS)
    par_ref[2:3, :] = as_row(gain_ref)
    par_ref[3:4, :] = as_row(shift_ref)


def back_finish_kernel(total, inverse, scaled, *refs):
    *parts, par_ref, back_ref, shift_ref, gain_ref = refs
    sums = parts[0][...]
    for p in parts[1:]:
        sums = sums + p[...]
    back_ref[0:1, :] = par_ref[0:1, :]
    back_ref[1:2, :] = par_ref[inverse : inverse + 1, :]
    back_ref[2:3, :] = par_ref[1:2, :] if scaled else par_ref[2:3, :] * par_ref[inverse : inverse + 1, :]
    back_ref[3:5, :] = sums * (1.0 / total)
    shift_ref[...] = sums[0]
    gain_ref[...] = sums[1]


def put_split(ref, top, left, value):
    rows = slice(top, top + value.shape[0])
    for half, part in enumerate(split(value)):
        start = left + half * (ref.shape[1] // 2)
        ref[rows, start : start + value.shape[1]] = part


def conv_kernel(x_ref, par_ref, taps_ref, act_ref, slope_ref, mid_ref, down_ref, up_ref, w_ref, sum_ref):
    windows, bins, channels = x_ref.shape
    mid = mid_ref.shape[2]
    rows = windows * bins

    @pl.when(pl.program_id(0) == 0)
    def _():
        for t in range(3):
            put_split(w_ref, 0, t * mid, taps_ref[t])

    for w in range(windows):
        for top in range(0, bins, 32):
            own = slice(top, top + 32)
            here = (x_ref[w, own, :] - par_ref[0:1, :]) * par_ref[1:2, :] + par_ref[2:3, :]
            value, slope = gelu_parts(here)
            slope_ref[w, own, :] = slope
            high, low = split(value)
            act_ref[w, own, 0:channels] = high
            act_ref[w, own, channels:] = low
    both = dot(act_ref[:, :, 0:channels].reshape(rows, channels), w_ref[...])
    rest = dot(act_ref[:, :, channels:].reshape(rows, channels), w_ref[:, : 3 * mid])
    sum_ref[...] = both[:, : 3 * mid] + both[:, 3 * mid :] + rest
    for w in range(windows):
        top, end = w * bins, (w + 1) * bins
        mid_ref[w] = sum_ref[top:end, mid : 2 * mid]
        mid_ref[w, STEP:, :] += sum_ref[top : end - STEP, 0:mid]
        mid_ref[w, : bins - STEP, :] += sum_ref[top + STEP : end, 2 * mid :]
        down_ref[w] = sum_ref[end - EDGE : end, 0:mid]
        up_ref[w] = sum_ref[top : top + EDGE, 2 * mid :]


def point_in_kernel(cot_ref, point_ref, out_ref, w_ref):
    windows, bins, channels = cot_ref.shape
    mid = out_ref.shape[2]

    @pl.when(pl.program_id(0) == 0)
    def _():
        put_split(w_ref, 0, 0, point_ref[...].T)

    high, low = split(cot_ref[...].reshape(windows * bins, channels))
    both = dot(high, w_ref[...])
    total = both[:, :mid] + both[:, mid:] + dot(low, w_ref[:, :mid])
    out_ref[...] = total.reshape(windows, bins, mid)


def second_moments_kernel(blocks, part_ref, above_ref, below_ref, *refs):
    *before, mid_ref, out_ref = refs
    windows, bins, mid = part_ref.shape
    step = pl.program_id(0)
    lead = EDGE - STEP
    for ref in before:

        @pl.when(step == 0)
        def _(ref=ref):
            out_ref[...] = ref[...]

    for w in range(windows):
        mid_ref[w] = part_ref[w]
        mid_ref[w, 0:STEP, :] += above_ref[w, lead:, :]
        mid_ref[w, bins - STEP :, :] += below_ref[w, 0:STEP, :]
    add_moments(out_ref, step + blocks, mid_ref, step + blocks == 0)


def eighths(value):
    return jnp.sum(value.reshape(value.shape[0] // 8, 8, value.shape[1]), axis=0)


def second_act_kernel(mid_ref, g_ref, par_ref, act_ref, up_ref, sums_ref, shift_ref, gain_ref):
    windows, bins, mid = mid_ref.shape
    step = pl.program_id(0)

    @pl.when(step == 0)
    def _():
        shift_ref[...] = jnp.zeros_like(shift_ref)
        gain_ref[...] = jnp.zeros_like(gain_ref)

    shift_sum, gain_sum = shift_ref[...], gain_ref[...]
    for w in range(windows):
        for top in range(0, bins, 32):
            own = slice(top, top + 32)
            normed = (mid_ref[w, own, :] - par_ref[0:1, :]) * par_ref[1:2, :]
            value, slope = gelu_parts(normed * par_ref[2:3, :] + par_ref[3:4, :])
            up = g_ref[w, own, :] * slope
            up_ref[w, own, :] = up
            high, low = split(value)
            act_ref[w, own, 0:mid] = high
            act_ref[w, own, mid:] = low
            shift_sum = shift_sum + eighths(up)
            gain_sum = gain_sum + eighths(up * normed)
    shift_ref[...] = shift_sum
    gain_ref[...] = gain_sum

    @pl.when(step == pl.num_programs(0) - 1)
    def _():
        sums_ref[0:1, :] = fold(shift_ref[...])
        sums_ref[1:2, :] = fold(gain_ref[...])


def point_grad_kernel(cot_ref, act_ref, out_ref, sum_ref):
    windows, bins, channels = cot_ref.shape
    mid = sum_ref.shape[0]
    rows = windows * bins
    step = pl.program_id(0)

    @pl.when(step == 0)
    def _():
        sum_ref[...] = jnp.zeros_like(sum_ref)

    act = act_ref[...].reshape(rows, 2 * mid)
    high, low = split(cot_ref[...].reshape(rows, channels))
    both = dot_rows(act, high)
    sum_ref[...] += both[:mid] + both[mid:] + dot_rows(act[:, :mid], low)

    @pl.when(step == pl.num_programs(0) - 1)
    def _():
        out_ref[0] = sum_ref[...].T


def point_out_kernel(x_ref, act_ref, point_ref, out_ref, w_ref):
    windows, bins, channels = x_ref.shape
    rows, mid = windows * bins, act_ref.shape[2] // 2

    @pl.when(pl.program_id(0) == 0)
    def _():
        high, low = split(point_ref[...])
        w_ref[0:mid, :] = high
        w_ref[mid : 2 * mid, :] = high
        w_ref[2 * mid :, :] = low

    act = act_ref[...].reshape(rows, 2 * mid)
    branch = dot(act, w_ref[0 : 2 * mid, :]) + dot(act[:, :mid], w_ref[2 * mid :, :])
    out_ref[...] = x_ref[...] + branch.reshape(windows, bins, channels)


def mid_grad(up, mid, par_ref):
    normed = (mid - par_ref[0:1, :]) * par_ref[1:2, :]
    return par_ref[2:3, :] * (up - par_ref[3:4, :] - normed * par_ref[4:5, :])


def edge_grad_kernel(up_first_ref, up_last_ref, mid_first_ref, mid_last_ref, par_ref, first_ref, last_ref):
    for w in range(first_ref.shape[0]):
        first_ref[w] = mid_grad(up_first_ref[w], mid_first_ref[w], par_ref)
        last_ref[w] = mid_grad(up_last_ref[w], mid_last_ref[w], par_ref)


def widen(grad_ref, above_ref, below_ref, wide_ref, w):
    bins = grad_ref.shape[1]
    wide_ref[0:EDGE, :] = above_ref[w]
    wide_ref[EDGE : EDGE + bins, :] = grad_ref[w]
    wide_ref[EDGE + bins :, :] = below_ref[w]


def middle_grad_kernel(up_ref, mid_ref, par_ref, act_ref, grad_ref, out_ref, sum_ref, taps_ref):
    windows, bins, mid = grad_ref.shape
    rows = windows * bins
    channels = act_ref.shape[2] // 2
    step = pl.program_id(0)

    @pl.when(step == 0)
    def _():
        sum_ref[...] = jnp.zeros_like(sum_ref)

    for w in range(windows):
        for top in range(0, bins, 64):
            own = slice(top, top + 64)
            grad = mid_grad(up_ref[w, own, :], mid_ref[w, own, :], par_ref)
            grad_ref[w, own, :] = grad
            put_split(taps_ref, w * bins + top, 0, grad)
    both = dot_rows(taps_ref[...], act_ref[:, :, 0:channels].reshape(rows, channels))
    rest = dot_rows(taps_ref[:, :mid], act_ref[:, :, channels:].reshape(rows, channels))
    sum_ref[...] += both[:mid] + both[mid:] + rest

    @pl.when(step == pl.num_programs(0) - 1)
    def _():
        out_ref[0] = sum_ref[...].T


def outer_grad_kernel(first, last, grad_ref, above_ref, below_ref, act_ref, *refs):
    if not first:
        before_ref, *refs = refs
    out_ref, sum_ref, taps_ref, wide_ref = refs
    windows, bins, mid = grad_ref.shape
    count = 2 * mid
    rows = windows * bins
    channels = act_ref.shape[2] // 2
    step = pl.program_id(0)
    end = pl.num_programs(0) - (2 if last else 1)

    @pl.when(step == 0)
    def _():
        sum_ref[...] = jnp.zeros_like(sum_ref) if first else before_ref[...]

    @pl.when(step <= end)
    def _():
        for w in range(windows):
            widen(grad_ref, above_ref, below_ref, wide_ref, w)
            for k, t in enumerate((0, 2)):
                start = EDGE + (1 - t) * STEP
                put_split(taps_ref, w * bins, k * mid, wide_ref[start : start + bins, :])
        both = dot_rows(act_ref[:, :, 0:channels].reshape(rows, channels), taps_ref[...])
        rest = dot_rows(act_ref[:, :, channels:].reshape(rows, channels), taps_ref[:, :count])
        sum_ref[...] += both[:, :count] + both[:, count:] + rest

    for k in range(2 if last else 1):

        @pl.when(step == end + k)
        def _(k=k):
            if last:
                out_ref[0] = sum_ref[:, k * mid : (k + 1) * mid]
            else:
                out_ref[...] = sum_ref[...]


def act_grad_kernel(first, grad_ref, above_ref, below_ref, slope_ref, x_ref, par_ref, kernel_ref, *refs):
    if not first:
        before_ref, *refs = refs
    up_ref, sums_ref, taps_ref, part_ref, wide_ref, w_ref, sum_ref = refs
    windows, bins, mid = grad_ref.shape
    channels = x_ref.shape[2]
    depth = 3 * mid
    step = pl.program_id(0)

    @pl.when(step == 0)
    def _():
        sums_ref[...] = jnp.zeros_like(sums_ref) if first else before_ref[...]
        part_ref[...] = jnp.zeros_like(part_ref)
        for t in range(3):
            high, low = split(kernel_ref[t].T)
            own = slice(t * mid, (t + 1) * mid)
            w_ref[own, :] = high
            w_ref[depth + t * mid : depth + (t + 1) * mid, :] = high
            w_ref[2 * depth + t * mid : 2 * depth + (t + 1) * mid, :] = low

    for w in range(windows):
        widen(grad_ref, above_ref, below_ref, wide_ref, w)
        for t in range(3):
            start = EDGE + (1 - t) * STEP
            put_split(taps_ref, w * bins, t * mid, wide_ref[start : start + bins, :])
    sum_ref[...] = dot(taps_ref[...], w_ref[0 : 2 * depth, :]) + dot(taps_ref[:, :depth], w_ref[2 * depth :, :])
    shift_sum, gain_sum = part_ref[0], part_ref[1]
    for w in range(windows):
        for top in range(0, bins, 32):
            own = slice(top, top + 32)
            up = sum_ref[w * bins + top : w * bins + top + 32, :] * slope_ref[w, own, :]
            up_ref[w, own, :] = up
            shift_sum = shift_sum + eighths(up)
            gain_sum = gain_sum + eighths(up * ((x_ref[w, own, :] - par_ref[0:1, :]) * par_ref[3:4, :]))
    part_ref[0] = shift_sum
    part_ref[1] = gain_sum

    @pl.when(step == pl.num_programs(0) - 1)
    def _():
        sums_ref[0:1, :] += fold(part_ref[0])
        sums_ref[1:2, :] += fold(part_ref[1])


def input_grad_kernel(cot_ref, up_ref, x_ref, par_ref, out_ref):
    center, inverse, scale, shift_mean, gain_mean = (par_ref[k : k + 1, :] for k in range(5))
    for w in range(cot_ref.shape[0]):
        normed = (x_ref[w] - center) * inverse
        out_ref[w] = cot_ref[w] + scale * (up_ref[w] - shift_mean - normed * gain_mean)


def on_device(x, first_gain, first_shift, taps, second_gain, second_shift, point, cot):
    windows, bins, channels = x.shape
    mid = point.shape[0]
    devices = lax.axis_size("seq") * lax.axis_size(DP)
    local = windows * bins
    total = float(local * devices)
    chunks = 2 if windows % 4 == 0 else 1
    per = windows // chunks
    pair = 2 if per % 2 == 0 else 1
    quad = 4 if per % 4 == 0 else pair
    steps = per // pair
    count = per // quad
    mac = 2 * local * channels * mid

    def own(a, offset=0, size=pair, index=None):
        rest = (0,) * (a.ndim - 1)
        return (a, (size,) + a.shape[1:], index or (lambda i: (i + offset,) + rest))

    def made(shape, dtype=F32, offset=0, size=pair, index=None):
        rest = (0,) * (len(shape) - 1)
        return (shape, dtype, (size,) + shape[1:], index or (lambda i: (i + offset,) + rest))

    def whole(a):
        return (a, None, None)

    def kept(*shape, dtype=F32):
        return (shape, dtype, None, None)

    moments = call(
        first_moments_kernel,
        (windows // quad,),
        [own(x, size=quad)],
        [kept(2, channels)],
        moved=x.size * 4,
    )[0]
    gathered = gather_moments(moments, local)
    first_par = call(
        functools.partial(first_finish_kernel, float(local * lax.axis_size(DP)), total),
        (),
        [whole(p) for p in gathered] + [whole(first_gain), whole(first_shift)],
        [kept(4, channels)],
    )[0]

    seq = lax.axis_size("seq")
    onward = [(i, i + 1) for i in range(seq - 1)]
    back = [(i + 1, i) for i in range(seq - 1)]

    full, aboves, belows = (), [], []
    for c in range(chunks):
        *full, down, up = call(
            conv_kernel,
            (steps,),
            [own(x, c * steps), whole(first_par), whole(taps)],
            [
                made((windows, bins, 2 * channels), BF16, c * steps),
                made((windows, bins, channels), F32, c * steps),
                made((windows, bins, mid), F32, c * steps),
                made((per, EDGE, mid)),
                made((per, EDGE, mid)),
            ],
            [pltpu.VMEM((channels, 6 * mid), BF16), pltpu.VMEM((pair * bins, 3 * mid), F32)],
            flops=9 * mac / chunks,
            moved=x.size * 14 / chunks,
            into=full,
        )
        aboves.append(lax.ppermute(down, "seq", onward))
        belows.append(lax.ppermute(up, "seq", back))
    act, slope, partial = full

    pulled = call(
        point_in_kernel,
        (windows // quad,),
        [own(cot, size=quad), whole(point)],
        [made((windows, bins, mid), size=quad)],
        [pltpu.VMEM((channels, 2 * mid), BF16)],
        flops=3 * mac,
        moved=x.size * 6,
        after=aboves[:-1] + belows[:-1] + [partial],
    )[0]

    mids, moments = (), ()
    for c in range(chunks):
        *mids, moment = call(
            functools.partial(second_moments_kernel, c * count),
            (count,),
            [own(partial, c * count, quad), own(aboves[c], 0, quad), own(belows[c], 0, quad)] + [whole(m) for m in moments],
            [made((windows, bins, mid), F32, c * count, quad), kept(2, mid)],
            moved=x.size * 5 / chunks,
            into=mids,
            after=[pulled] if c == chunks - 1 else (),
        )
        moments = [moment]
    mids = mids[0]
    gathered = gather_moments(moment, local)
    second_par = call(
        functools.partial(second_finish_kernel, float(local * lax.axis_size(DP)), total),
        (),
        [whole(p) for p in gathered] + [whole(second_gain), whole(second_shift)],
        [kept(4, mid)],
    )[0]
    second_act, ups, sums = call(
        second_act_kernel,
        (windows // quad,),
        [own(mids, size=quad), own(pulled, size=quad), whole(second_par)],
        [made((windows, bins, 2 * mid), BF16, size=quad), made((windows, bins, mid), size=quad), kept(2, mid)],
        [pltpu.VMEM((8, mid), F32)] * 2,
        moved=x.size * 8,
    )
    gathered = gather_sums(sums)

    weight_grads = call(
        point_grad_kernel,
        (windows // quad,),
        [own(cot, size=quad), own(second_act, size=quad)],
        [made((4, channels, mid), size=1, index=lambda i: (3, 0, 0))],
        [pltpu.VMEM((mid, channels), F32)],
        flops=3 * mac,
        moved=x.size * 6,
    )

    back_par, second_shift_grad, second_gain_grad = call(
        functools.partial(back_finish_kernel, total, 1, False),
        (),
        [whole(p) for p in gathered] + [whole(second_par)],
        [kept(5, mid), kept(mid), kept(mid)],
        after=weight_grads,
    )
    grad_aboves, grad_belows = [], []
    tail = bins // EDGE - 1
    for c in range(chunks):
        edge = (quad, EDGE, mid)
        places = [lambda i, c=c, b=b: (i + c * count, b, 0) for b in (0, tail)]
        first, last = call(
            edge_grad_kernel,
            (count,),
            [(a, edge, place) for a in (ups, mids) for place in places] + [whole(back_par)],
            [made((per, EDGE, mid), size=quad), made((per, EDGE, mid), size=quad)],
            moved=x.size * 2 / chunks,
        )
        grad_aboves.append(lax.ppermute(last, "seq", onward))
        grad_belows.append(lax.ppermute(first, "seq", back))

    wide = [pltpu.VMEM((bins + 2 * EDGE, mid), F32)]
    grads, *weight_grads = call(
        middle_grad_kernel,
        (windows // quad,),
        [own(ups, size=quad), own(mids, size=quad), whole(back_par), own(act, size=quad)],
        [
            made((windows, bins, mid), size=quad),
            made((4, channels, mid), size=1, index=lambda i: (1, 0, 0)),
        ],
        [pltpu.VMEM((mid, channels), F32), pltpu.VMEM((quad * bins, 2 * mid), BF16)],
        flops=3 * mac,
        moved=x.size * 10,
        into=weight_grads,
        into_first=1,
    )
    outer = ()
    for c in range(chunks):
        end = c == chunks - 1

        def at(c=c, first=0):
            return lambda i: (jnp.minimum(i, count - 1) + first, 0, 0)

        outer = call(
            functools.partial(outer_grad_kernel, c == 0, end),
            (count + end,),
            [
                own(grads, size=quad, index=at(first=c * count)),
                own(grad_aboves[c], size=quad, index=at()),
                own(grad_belows[c], size=quad, index=at()),
                own(act, size=quad, index=at(first=c * count)),
            ]
            + [whole(o) for o in outer],
            [
                made((4, channels, mid), size=1, index=lambda i: (jnp.where(i >= count, 2, 0), 0, 0))
                if end
                else kept(channels, 2 * mid)
            ],
            [pltpu.VMEM((channels, 2 * mid), F32), pltpu.VMEM((quad * bins, 4 * mid), BF16)] + wide,
            flops=6 * mac / chunks,
            moved=x.size * 8 / chunks,
            into=weight_grads if end else (),
            after=weight_grads if c == 0 else (),
        )
    scattered = lax.psum_scatter(outer[0], DP, scatter_dimension=1, tiled=True)

    block_output = call(
        point_out_kernel,
        (windows // quad,),
        [own(x, size=quad), own(second_act, size=quad), whole(point)],
        [made((windows, bins, channels), size=quad)],
        [pltpu.VMEM((3 * mid, channels), BF16)],
        flops=3 * mac,
        moved=x.size * 10,
        after=outer[:1],
    )[0]

    sums, first_up = (), ()
    for c in range(chunks):
        *first_up, last = call(
            functools.partial(act_grad_kernel, c == 0),
            (steps,),
            [
                own(grads, c * steps),
                own(grad_aboves[c]),
                own(grad_belows[c]),
                own(slope, c * steps),
                own(x, c * steps),
                whole(first_par),
                whole(taps),
            ]
            + [whole(s) for s in sums],
            [made((windows, bins, channels), F32, c * steps), kept(2, channels)],
            [
                pltpu.VMEM((pair * bins, 6 * mid), BF16),
                pltpu.VMEM((2, 8, channels), F32),
                pltpu.VMEM((bins + 2 * EDGE, mid), F32),
                pltpu.VMEM((9 * mid, channels), BF16),
                pltpu.VMEM((pair * bins, channels), F32),
            ],
            flops=9 * mac / chunks,
            moved=x.size * 14 / chunks,
            into=first_up,
            after=[block_output] if c == 0 else (),
        )
        sums = [last]
        if c == 0:
            scattered = lax.psum(lax.optimization_barrier((scattered, last))[0], "seq")
    half_summed = functools.reduce(jnp.add, peers(last, DP))
    gathered = peers(half_summed, "seq")
    last_par, first_shift_grad, first_gain_grad = call(
        functools.partial(back_finish_kernel, total, 3, True),
        (),
        [whole(p) for p in gathered] + [whole(first_par)],
        [kept(5, channels), kept(channels), kept(channels)],
    )
    scattered = lax.optimization_barrier((scattered, half_summed))[0]
    total_grads = lax.all_gather(scattered, DP, axis=1, tiled=True)
    tap_grad = total_grads[:3]
    point_grad = total_grads[3].T
    input_grad = call(
        input_grad_kernel,
        (windows // quad,),
        [own(cot, size=quad), own(first_up[0], size=quad), own(x, size=quad), whole(last_par)],
        [made((windows, bins, channels), size=quad)],
        moved=x.size * 16,
    )[0]
    return (
        block_output,
        input_grad,
        first_gain_grad,
        first_shift_grad,
        tap_grad,
        second_gain_grad,
        second_shift_grad,
        point_grad,
    )


def solution(mesh):
    seq, dp = mesh.devices.shape
    split_mesh = Mesh(mesh.devices.reshape(seq, dp // 2, 2), ("seq",) + DP)
    rows = P(DP, "seq", None)
    return jax.shard_map(
        on_device,
        mesh=split_mesh,
        in_specs=(rows, P(), P(), P(), P(), P(), P(), rows),
        out_specs=(rows, rows, P(), P(), P(), P(), P(), P()),
        check_vma=False,
    )
```

```python
import functools

import jax
import jax.numpy as jnp
from jax import lax
from jax.experimental import pallas as pl
from jax.experimental.pallas import tpu as pltpu
from jax.sharding import Mesh
from jax.sharding import PartitionSpec as P

STEP = 57
EDGE = 64
EPS = 1e-05
LOG2_INV_ROOT_TWO_PI = -1.3257480647361592
HALF_LOG2_E = 0.7213475204444817
MIB = 1024 * 1024
F32 = jnp.float32
BF16 = jnp.bfloat16
DP = ("chip", "core")

PHI = (
    0.7978849414599987,
    0.03633308457510501,
    -3.2594975844072696e-05,
    -5.530619400541097e-05,
    3.964744542062183e-06,
    -1.3226335479189098e-07,
    1.7561713084457843e-09,
)


def gelu_parts(v):
    square = v * v
    poly = PHI[6]
    for k in (5, 4, 3, 2, 1, 0):
        poly = poly * square + PHI[k]
    cdf = 0.5 * jnp.tanh(v * poly) + 0.5
    return v * cdf, cdf + v * jnp.exp2(square * (-HALF_LOG2_E) + LOG2_INV_ROOT_TWO_PI)


def split(v):
    high = v.astype(BF16)
    return high, (v - high.astype(F32)).astype(BF16)


def fold(x):
    return jnp.sum(x, axis=0, keepdims=True)


def dot(left, right):
    return lax.dot_general(left, right, (((1,), (0,)), ((), ())), preferred_element_type=F32)


def dot_rows(left, right):
    return lax.dot_general(left, right, (((0,), (0,)), ((), ())), preferred_element_type=F32)


def call(kernel, grid, ins, outs, scratch=(), vmem=60, flops=0, moved=0, into=(), after=()):
    hold = list(after) + list(into)
    aliases = {len(ins) + len(after) + k: k for k in range(len(into))}

    def body(*refs):
        kernel(*refs[: len(ins)], *refs[len(ins) + len(hold) :])

    def spec(shape, block, index, keep):
        if block is None:
            return pl.BlockSpec(shape, lambda *i: (0,) * len(shape), pipeline_mode=pl.Buffered(1) if keep else None)
        return pl.BlockSpec(block, index)

    return pl.pallas_call(
        body,
        grid=grid,
        in_specs=[spec(a.shape, b, i, True) for a, b, i in ins] + [pl.BlockSpec(memory_space=pltpu.HBM)] * len(hold),
        out_specs=[spec(s, b, i, False) for s, _, b, i in outs],
        out_shape=[jax.ShapeDtypeStruct(s, d) for s, d, _, _ in outs],
        scratch_shapes=list(scratch),
        compiler_params=pltpu.CompilerParams(vmem_limit_bytes=vmem * MIB),
        input_output_aliases=aliases,
        cost_estimate=pl.CostEstimate(flops=int(flops), bytes_accessed=int(moved), transcendentals=0),
    )(*[a for a, _, _ in ins], *hold)


def add_moments(out_ref, blocks, ref, fresh):
    windows, bins, channels = ref.shape
    rows = windows * bins

    total = eighths(ref[0])
    for w in range(1, windows):
        total = total + eighths(ref[w])
    mean = fold(total) * (1.0 / rows)
    square = None
    for w in range(windows):
        off = ref[w] - mean
        square = eighths(off * off) if square is None else square + eighths(off * off)
    square = fold(square)

    @pl.when(fresh)
    def _():
        out_ref[0:1, :] = mean
        out_ref[1:2, :] = square

    @pl.when(jnp.logical_not(fresh))
    def _():
        n = lax.convert_element_type(blocks, F32)
        share = 1.0 / (n + 1.0)
        delta = mean - out_ref[0:1, :]
        out_ref[0:1, :] = out_ref[0:1, :] + delta * share
        out_ref[1:2, :] = out_ref[1:2, :] + square + delta * delta * (rows * n * share)


def merge_moments(parts, count):
    mean = parts[0][0:1, :]
    for p in parts[1:]:
        mean = mean + p[0:1, :]
    mean = mean * (1.0 / len(parts))
    square = jnp.zeros_like(mean)
    for p in parts:
        off = p[0:1, :] - mean
        square = square + (p[1:2, :] + (off * off) * count)
    return mean, square


def merge_moments_kernel(count, *refs):
    *parts, out_ref = refs
    mean, square = merge_moments(parts, count)
    out_ref[0:1, :] = mean
    out_ref[1:2, :] = square


def peers(array, axis):
    count = lax.axis_size(axis)
    return [array] + [
        lax.ppermute(array, axis, [(i, (i + by) % count) for i in range(count)]) for by in range(1, count)
    ]


def gather_moments(moments, count):
    merged = call(
        functools.partial(merge_moments_kernel, float(count)),
        (),
        [(p, None, None) for p in peers(moments, DP)],
        [(moments.shape, F32, None, None)],
    )[0]
    return peers(merged, "seq")


def gather_sums(sums):
    return peers(functools.reduce(jnp.add, peers(sums, DP)), "seq")


def first_moments_kernel(x_ref, out_ref):
    step = pl.program_id(0)
    add_moments(out_ref, step, x_ref, step == 0)


def as_row(ref):
    return ref[...].reshape(1, ref.shape[0])


def first_finish(count, total, *refs):
    *parts, gain_ref, shift_ref, par_ref = refs
    mean, square = merge_moments(parts, count)
    inverse = lax.rsqrt(square * (1.0 / total) + EPS)
    par_ref[0:1, :] = mean
    par_ref[1:2, :] = as_row(gain_ref) * inverse
    par_ref[2:3, :] = as_row(shift_ref)
    par_ref[3:4, :] = inverse


def second_finish(count, total, *refs):
    *parts, gain_ref, shift_ref, par_ref = refs
    mean, square = merge_moments(parts, count)
    par_ref[0:1, :] = mean
    par_ref[1:2, :] = lax.rsqrt(square * (1.0 / total) + EPS)
    par_ref[2:3, :] = as_row(gain_ref)
    par_ref[3:4, :] = as_row(shift_ref)


def back_finish(total, inverse, scaled, *refs):
    *parts, par_ref, back_ref, shift_ref, gain_ref = refs
    sums = parts[0][...]
    for p in parts[1:]:
        sums = sums + p[...]
    back_ref[0:1, :] = par_ref[0:1, :]
    back_ref[1:2, :] = par_ref[inverse : inverse + 1, :]
    back_ref[2:3, :] = par_ref[1:2, :] if scaled else par_ref[2:3, :] * par_ref[inverse : inverse + 1, :]
    back_ref[3:5, :] = sums * (1.0 / total)
    shift_ref[...] = sums[0]
    gain_ref[...] = sums[1]


def put_split(ref, top, left, value):
    rows = slice(top, top + value.shape[0])
    for half, part in enumerate(split(value)):
        start = left + half * (ref.shape[1] // 2)
        ref[rows, start : start + value.shape[1]] = part


def conv_kernel(finish, x_ref, taps_ref, *refs):
    if finish is None:
        par_ref, *refs = refs
        act_ref, slope_ref, mid_ref, down_ref, up_ref, w_ref, sum_ref = refs
    else:
        *raw, act_ref, slope_ref, mid_ref, down_ref, up_ref, par_ref, w_ref, sum_ref = refs
    windows, bins, channels = x_ref.shape
    mid = mid_ref.shape[2]
    rows = windows * bins

    @pl.when(pl.program_id(0) == 0)
    def _():
        if finish is not None:
            finish(*raw, par_ref)
        for t in range(3):
            put_split(w_ref, 0, t * mid, taps_ref[t])

    for w in range(windows):
        for top in range(0, bins, 32):
            own = slice(top, top + 32)
            here = (x_ref[w, own, :] - par_ref[0:1, :]) * par_ref[1:2, :] + par_ref[2:3, :]
            value, slope = gelu_parts(here)
            slope_ref[w, own, :] = slope
            high, low = split(value)
            act_ref[w, own, 0:channels] = high
            act_ref[w, own, channels:] = low
    both = dot(act_ref[:, :, 0:channels].reshape(rows, channels), w_ref[...])
    rest = dot(act_ref[:, :, channels:].reshape(rows, channels), w_ref[:, : 3 * mid])
    sum_ref[...] = both[:, : 3 * mid] + both[:, 3 * mid :] + rest
    for w in range(windows):
        top, end = w * bins, (w + 1) * bins
        mid_ref[w] = sum_ref[top:end, mid : 2 * mid]
        mid_ref[w, STEP:, :] += sum_ref[top : end - STEP, 0:mid]
        mid_ref[w, : bins - STEP, :] += sum_ref[top + STEP : end, 2 * mid :]
        down_ref[w] = sum_ref[end - EDGE : end, 0:mid]
        up_ref[w] = sum_ref[top : top + EDGE, 2 * mid :]


def point_in_kernel(cot_ref, point_ref, out_ref, w_ref):
    windows, bins, channels = cot_ref.shape
    mid = out_ref.shape[2]

    @pl.when(pl.program_id(0) == 0)
    def _():
        put_split(w_ref, 0, 0, point_ref[...].T)

    high, low = split(cot_ref[...].reshape(windows * bins, channels))
    both = dot(high, w_ref[...])
    total = both[:, :mid] + both[:, mid:] + dot(low, w_ref[:, :mid])
    out_ref[...] = total.reshape(windows, bins, mid)


def second_moments_kernel(blocks, part_ref, above_ref, below_ref, *refs):
    *before, mid_ref, out_ref = refs
    windows, bins, mid = part_ref.shape
    step = pl.program_id(0)
    lead = EDGE - STEP
    for ref in before:

        @pl.when(step == 0)
        def _(ref=ref):
            out_ref[...] = ref[...]

    for w in range(windows):
        mid_ref[w] = part_ref[w]
        mid_ref[w, 0:STEP, :] += above_ref[w, lead:, :]
        mid_ref[w, bins - STEP :, :] += below_ref[w, 0:STEP, :]
    add_moments(out_ref, step + blocks, mid_ref, step + blocks == 0)


def eighths(value):
    return jnp.sum(value.reshape(value.shape[0] // 8, 8, value.shape[1]), axis=0)


def point_in_moments_kernel(
    cot_ref, point_ref, part_ref, above_ref, below_ref, out_ref, mid_ref, moments_ref, w_ref
):
    point_in_kernel(cot_ref, point_ref, out_ref, w_ref)
    second_moments_kernel(0, part_ref, above_ref, below_ref, mid_ref, moments_ref)


def second_act_kernel(finish, mid_ref, g_ref, *refs):
    *raw, act_ref, up_ref, sums_ref, par_ref, shift_ref, gain_ref = refs
    windows, bins, mid = mid_ref.shape
    step = pl.program_id(0)

    @pl.when(step == 0)
    def _():
        finish(*raw, par_ref)
        shift_ref[...] = jnp.zeros_like(shift_ref)
        gain_ref[...] = jnp.zeros_like(gain_ref)

    shift_sum, gain_sum = shift_ref[...], gain_ref[...]
    for w in range(windows):
        for top in range(0, bins, 32):
            own = slice(top, top + 32)
            normed = (mid_ref[w, own, :] - par_ref[0:1, :]) * par_ref[1:2, :]
            value, slope = gelu_parts(normed * par_ref[2:3, :] + par_ref[3:4, :])
            up = g_ref[w, own, :] * slope
            up_ref[w, own, :] = up
            high, low = split(value)
            act_ref[w, own, 0:mid] = high
            act_ref[w, own, mid:] = low
            shift_sum = shift_sum + eighths(up)
            gain_sum = gain_sum + eighths(up * normed)
    shift_ref[...] = shift_sum
    gain_ref[...] = gain_sum

    @pl.when(step == pl.num_programs(0) - 1)
    def _():
        sums_ref[0:1, :] = fold(shift_ref[...])
        sums_ref[1:2, :] = fold(gain_ref[...])


def point_grad_kernel(cot_ref, act_ref, out_ref, sum_ref):
    windows, bins, channels = cot_ref.shape
    mid = sum_ref.shape[0]
    rows = windows * bins
    step = pl.program_id(0)

    @pl.when(step == 0)
    def _():
        sum_ref[...] = jnp.zeros_like(sum_ref)

    act = act_ref[...].reshape(rows, 2 * mid)
    high, low = split(cot_ref[...].reshape(rows, channels))
    both = dot_rows(act, high)
    sum_ref[...] += both[:mid] + both[mid:] + dot_rows(act[:, :mid], low)

    @pl.when(step == pl.num_programs(0) - 1)
    def _():
        out_ref[0] = sum_ref[...].T


def point_out_kernel(x_ref, act_ref, point_ref, out_ref, w_ref):
    windows, bins, channels = x_ref.shape
    rows, mid = windows * bins, act_ref.shape[2] // 2

    @pl.when(pl.program_id(0) == 0)
    def _():
        high, low = split(point_ref[...])
        w_ref[0:mid, :] = high
        w_ref[mid : 2 * mid, :] = high
        w_ref[2 * mid :, :] = low

    act = act_ref[...].reshape(rows, 2 * mid)
    branch = dot(act, w_ref[0 : 2 * mid, :]) + dot(act[:, :mid], w_ref[2 * mid :, :])
    out_ref[...] = x_ref[...] + branch.reshape(windows, bins, channels)


def mid_grad(up, mid, par_ref):
    normed = (mid - par_ref[0:1, :]) * par_ref[1:2, :]
    return par_ref[2:3, :] * (up - par_ref[3:4, :] - normed * par_ref[4:5, :])


def edge_grad_kernel(finish, up_first_ref, up_last_ref, mid_first_ref, mid_last_ref, *refs):
    if finish is None:
        par_ref, first_ref, last_ref = refs
    else:
        *raw, first_ref, last_ref, par_ref, shift_ref, gain_ref = refs

        @pl.when(pl.program_id(0) == 0)
        def _():
            finish(*raw, par_ref, shift_ref, gain_ref)

    for w in range(first_ref.shape[0]):
        first_ref[w] = mid_grad(up_first_ref[w], mid_first_ref[w], par_ref)
        last_ref[w] = mid_grad(up_last_ref[w], mid_last_ref[w], par_ref)


def widen(grad_ref, above_ref, below_ref, wide_ref, w):
    bins = grad_ref.shape[1]
    wide_ref[0:EDGE, :] = above_ref[w]
    wide_ref[EDGE : EDGE + bins, :] = grad_ref[w]
    wide_ref[EDGE + bins :, :] = below_ref[w]


def middle_grad_kernel(up_ref, mid_ref, par_ref, act_ref, grad_ref, out_ref, sum_ref, taps_ref):
    windows, bins, mid = grad_ref.shape
    rows = windows * bins
    channels = act_ref.shape[2] // 2
    step = pl.program_id(0)

    @pl.when(step == 0)
    def _():
        sum_ref[...] = jnp.zeros_like(sum_ref)

    for w in range(windows):
        for top in range(0, bins, 64):
            own = slice(top, top + 64)
            grad = mid_grad(up_ref[w, own, :], mid_ref[w, own, :], par_ref)
            grad_ref[w, own, :] = grad
            put_split(taps_ref, w * bins + top, 0, grad)
    both = dot_rows(taps_ref[...], act_ref[:, :, 0:channels].reshape(rows, channels))
    rest = dot_rows(taps_ref[:, :mid], act_ref[:, :, channels:].reshape(rows, channels))
    sum_ref[...] += both[:mid] + both[mid:] + rest

    @pl.when(step == pl.num_programs(0) - 1)
    def _():
        out_ref[0] = sum_ref[...].T


def outer_grad_kernel(first, last, grad_ref, above_ref, below_ref, act_ref, *refs):
    if not first:
        before_ref, *refs = refs
    out_ref, sum_ref, taps_ref, wide_ref = refs
    windows, bins, mid = grad_ref.shape
    count = 2 * mid
    rows = windows * bins
    channels = act_ref.shape[2] // 2
    step = pl.program_id(0)
    end = pl.num_programs(0) - (2 if last else 1)

    @pl.when(step == 0)
    def _():
        sum_ref[...] = jnp.zeros_like(sum_ref) if first else before_ref[...]

    @pl.when(step <= end)
    def _():
        for w in range(windows):
            widen(grad_ref, above_ref, below_ref, wide_ref, w)
            for k, t in enumerate((0, 2)):
                start = EDGE + (1 - t) * STEP
                put_split(taps_ref, w * bins, k * mid, wide_ref[start : start + bins, :])
        both = dot_rows(act_ref[:, :, 0:channels].reshape(rows, channels), taps_ref[...])
        rest = dot_rows(act_ref[:, :, channels:].reshape(rows, channels), taps_ref[:, :count])
        sum_ref[...] += both[:, :count] + both[:, count:] + rest

    for k in range(2 if last else 1):

        @pl.when(step == end + k)
        def _(k=k):
            if last:
                out_ref[0] = sum_ref[:, k * mid : (k + 1) * mid]
            else:
                out_ref[...] = sum_ref[...]


def act_grad_kernel(first, grad_ref, above_ref, below_ref, slope_ref, x_ref, par_ref, kernel_ref, *refs):
    if not first:
        before_ref, *refs = refs
    up_ref, sums_ref, taps_ref, part_ref, wide_ref, w_ref, sum_ref = refs
    windows, bins, mid = grad_ref.shape
    channels = x_ref.shape[2]
    depth = 3 * mid
    step = pl.program_id(0)

    @pl.when(step == 0)
    def _():
        sums_ref[...] = jnp.zeros_like(sums_ref) if first else before_ref[...]
        part_ref[...] = jnp.zeros_like(part_ref)
        for t in range(3):
            high, low = split(kernel_ref[t].T)
            own = slice(t * mid, (t + 1) * mid)
            w_ref[own, :] = high
            w_ref[depth + t * mid : depth + (t + 1) * mid, :] = high
            w_ref[2 * depth + t * mid : 2 * depth + (t + 1) * mid, :] = low

    for w in range(windows):
        widen(grad_ref, above_ref, below_ref, wide_ref, w)
        for t in range(3):
            start = EDGE + (1 - t) * STEP
            put_split(taps_ref, w * bins, t * mid, wide_ref[start : start + bins, :])
    sum_ref[...] = dot(taps_ref[...], w_ref[0 : 2 * depth, :]) + dot(taps_ref[:, :depth], w_ref[2 * depth :, :])
    shift_sum, gain_sum = part_ref[0], part_ref[1]
    for w in range(windows):
        for top in range(0, bins, 32):
            own = slice(top, top + 32)
            up = sum_ref[w * bins + top : w * bins + top + 32, :] * slope_ref[w, own, :]
            up_ref[w, own, :] = up
            shift_sum = shift_sum + eighths(up)
            gain_sum = gain_sum + eighths(up * ((x_ref[w, own, :] - par_ref[0:1, :]) * par_ref[3:4, :]))
    part_ref[0] = shift_sum
    part_ref[1] = gain_sum

    @pl.when(step == pl.num_programs(0) - 1)
    def _():
        sums_ref[0:1, :] += fold(part_ref[0])
        sums_ref[1:2, :] += fold(part_ref[1])


def input_grad_kernel(finish, cot_ref, up_ref, x_ref, *refs):
    *raw, out_ref, shift_ref, gain_ref, par_ref = refs

    @pl.when(pl.program_id(0) == 0)
    def _():
        finish(*raw, par_ref, shift_ref, gain_ref)

    center, inverse, scale, shift_mean, gain_mean = (par_ref[k : k + 1, :] for k in range(5))
    for w in range(cot_ref.shape[0]):
        normed = (x_ref[w] - center) * inverse
        out_ref[w] = cot_ref[w] + scale * (up_ref[w] - shift_mean - normed * gain_mean)


def on_device(x, first_gain, first_shift, taps, second_gain, second_shift, point, cot):
    windows, bins, channels = x.shape
    mid = point.shape[0]
    devices = lax.axis_size("seq") * lax.axis_size(DP)
    local = windows * bins
    total = float(local * devices)
    chunks = 2 if windows % 4 == 0 else 1
    per = windows // chunks
    pair = 2 if per % 2 == 0 else 1
    quad = 4 if per % 4 == 0 else pair
    steps = per // pair
    count = per // quad
    mac = 2 * local * channels * mid

    def own(a, offset=0, size=pair, index=None):
        rest = (0,) * (a.ndim - 1)
        return (a, (size,) + a.shape[1:], index or (lambda i: (i + offset,) + rest))

    def made(shape, dtype=F32, offset=0, size=pair, index=None):
        rest = (0,) * (len(shape) - 1)
        return (shape, dtype, (size,) + shape[1:], index or (lambda i: (i + offset,) + rest))

    def whole(a):
        return (a, None, None)

    def kept(*shape, dtype=F32):
        return (shape, dtype, None, None)

    moments = call(
        first_moments_kernel,
        (windows // quad,),
        [own(x, size=quad)],
        [kept(2, channels)],
        moved=x.size * 4,
    )[0]
    gathered = gather_moments(moments, local)
    first_finish_here = functools.partial(first_finish, float(local * lax.axis_size(DP)), total)
    first_raw = [whole(p) for p in gathered] + [whole(first_gain), whole(first_shift)]

    seq = lax.axis_size("seq")
    onward = [(i, i + 1) for i in range(seq - 1)]
    back = [(i + 1, i) for i in range(seq - 1)]

    full, aboves, belows = (), [], []
    for c in range(chunks):
        *full, down, up = call(
            functools.partial(conv_kernel, None if c else first_finish_here),
            (steps,),
            [own(x, c * steps), whole(taps)] + ([whole(first_par)] if c else first_raw),
            [
                made((windows, bins, 2 * channels), BF16, c * steps),
                made((windows, bins, channels), F32, c * steps),
                made((windows, bins, mid), F32, c * steps),
                made((per, EDGE, mid)),
                made((per, EDGE, mid)),
            ]
            + ([] if c else [kept(4, channels)]),
            [pltpu.VMEM((channels, 6 * mid), BF16), pltpu.VMEM((pair * bins, 3 * mid), F32)],
            flops=9 * mac / chunks,
            moved=x.size * 14 / chunks,
            into=full,
        )
        if c == 0:
            down, up, first_par = full[3], down, up
            full = full[:3]
        aboves.append(lax.ppermute(down, "seq", onward))
        belows.append(lax.ppermute(up, "seq", back))
    act, slope, partial = full

    first_steps = windows // quad
    small = per // first_steps if per % first_steps == 0 else per
    pulled, mids, moment = call(
        point_in_moments_kernel,
        (first_steps,),
        [
            own(cot, size=quad),
            whole(point),
            own(partial, size=small),
            own(aboves[0], size=small),
            own(belows[0], size=small),
        ],
        [made((windows, bins, mid), size=quad), made((windows, bins, mid), size=small), kept(2, mid)],
        [pltpu.VMEM((channels, 2 * mid), BF16)],
        flops=3 * mac,
        moved=x.size * 8,
    )

    mids = [mids]
    for c in range(1, chunks):
        *mids, moment = call(
            functools.partial(second_moments_kernel, c * count),
            (count,),
            [own(partial, c * count, quad), own(aboves[c], 0, quad), own(belows[c], 0, quad), whole(moment)],
            [made((windows, bins, mid), F32, c * count, quad), kept(2, mid)],
            moved=x.size * 5 / chunks,
            into=mids,
            after=[pulled],
        )
    mids = mids[0]
    gathered = gather_moments(moment, local)
    second_finish_here = functools.partial(second_finish, float(local * lax.axis_size(DP)), total)
    second_raw = [whole(p) for p in gathered] + [whole(second_gain), whole(second_shift)]
    second_act, ups, sums, second_par = call(
        functools.partial(second_act_kernel, second_finish_here),
        (windows // quad,),
        [own(mids, size=quad), own(pulled, size=quad)] + second_raw,
        [made((windows, bins, 2 * mid), BF16, size=quad), made((windows, bins, mid), size=quad), kept(2, mid), kept(4, mid)],
        [pltpu.VMEM((8, mid), F32)] * 2,
        moved=x.size * 8,
    )
    gathered = gather_sums(sums)

    weight_grads = call(
        point_grad_kernel,
        (windows // quad,),
        [own(cot, size=quad), own(second_act, size=quad)],
        [kept(1, channels, mid)],
        [pltpu.VMEM((mid, channels), F32)],
        flops=3 * mac,
        moved=x.size * 6,
    )

    early = lax.psum_scatter(weight_grads[0], DP, scatter_dimension=1, tiled=True)

    back_finish_here = functools.partial(back_finish, total, 1, False)
    back_raw = [whole(p) for p in gathered] + [whole(second_par)]
    grad_aboves, grad_belows = [], []
    tail = bins // EDGE - 1
    for c in range(chunks):
        edge = (quad, EDGE, mid)
        places = [lambda i, c=c, b=b: (i + c * count, b, 0) for b in (0, tail)]
        first, last, *more = call(
            functools.partial(edge_grad_kernel, None if c else back_finish_here),
            (count,),
            [(a, edge, place) for a in (ups, mids) for place in places] + ([whole(back_par)] if c else back_raw),
            [made((per, EDGE, mid), size=quad), made((per, EDGE, mid), size=quad)]
            + ([] if c else [kept(5, mid), kept(mid), kept(mid)]),
            moved=x.size * 2 / chunks,
            after=() if c else weight_grads,
        )
        if c == 0:
            back_par, second_shift_grad, second_gain_grad = more
        grad_aboves.append(lax.ppermute(last, "seq", onward))
        grad_belows.append(lax.ppermute(first, "seq", back))

    wide = [pltpu.VMEM((bins + 2 * EDGE, mid), F32)]
    grads, *tap_grads = call(
        middle_grad_kernel,
        (windows // quad,),
        [own(ups, size=quad), own(mids, size=quad), whole(back_par), own(act, size=quad)],
        [
            made((windows, bins, mid), size=quad),
            made((3, channels, mid), size=1, index=lambda i: (1, 0, 0)),
        ],
        [pltpu.VMEM((mid, channels), F32), pltpu.VMEM((quad * bins, 2 * mid), BF16)],
        flops=3 * mac,
        moved=x.size * 10,
        after=[first, last],
    )
    outer = ()
    for c in range(chunks):
        end = c == chunks - 1

        def at(c=c, first=0):
            return lambda i: (jnp.minimum(i, count - 1) + first, 0, 0)

        outer = call(
            functools.partial(outer_grad_kernel, c == 0, end),
            (count + end,),
            [
                own(grads, size=quad, index=at(first=c * count)),
                own(grad_aboves[c], size=quad, index=at()),
                own(grad_belows[c], size=quad, index=at()),
                own(act, size=quad, index=at(first=c * count)),
            ]
            + [whole(o) for o in outer],
            [
                made((3, channels, mid), size=1, index=lambda i: (jnp.where(i >= count, 2, 0), 0, 0))
                if end
                else kept(channels, 2 * mid)
            ],
            [pltpu.VMEM((channels, 2 * mid), F32), pltpu.VMEM((quad * bins, 4 * mid), BF16)] + wide,
            flops=6 * mac / chunks,
            moved=x.size * 8 / chunks,
            into=tap_grads if end else (),
            after=tap_grads if c == 0 else (),
        )
    late = lax.optimization_barrier((outer[0], early))[0]
    late = lax.psum_scatter(late, DP, scatter_dimension=1, tiled=True)
    scattered = jnp.concatenate([late, early], axis=0)

    block_output = call(
        point_out_kernel,
        (windows // quad,),
        [own(x, size=quad), own(second_act, size=quad), whole(point)],
        [made((windows, bins, channels), size=quad)],
        [pltpu.VMEM((3 * mid, channels), BF16)],
        flops=3 * mac,
        moved=x.size * 10,
        after=outer[:1],
    )[0]

    sums, first_up = (), ()
    for c in range(chunks):
        *first_up, last = call(
            functools.partial(act_grad_kernel, c == 0),
            (steps,),
            [
                own(grads, c * steps),
                own(grad_aboves[c]),
                own(grad_belows[c]),
                own(slope, c * steps),
                own(x, c * steps),
                whole(first_par),
                whole(taps),
            ]
            + [whole(s) for s in sums],
            [made((windows, bins, channels), F32, c * steps), kept(2, channels)],
            [
                pltpu.VMEM((pair * bins, 6 * mid), BF16),
                pltpu.VMEM((2, 8, channels), F32),
                pltpu.VMEM((bins + 2 * EDGE, mid), F32),
                pltpu.VMEM((9 * mid, channels), BF16),
                pltpu.VMEM((pair * bins, channels), F32),
            ],
            flops=9 * mac / chunks,
            moved=x.size * 14 / chunks,
            into=first_up,
            after=[block_output] if c == 0 else (),
        )
        sums = [last]
        if c == 0:
            scattered = lax.psum(lax.optimization_barrier((scattered, last))[0], "seq")
    half_summed = functools.reduce(jnp.add, peers(last, DP))
    gathered = peers(half_summed, "seq")
    scattered = lax.optimization_barrier((scattered, half_summed))[0]
    total_grads = lax.all_gather(scattered, DP, axis=1, tiled=True)
    tap_grad = total_grads[:3]
    point_grad = total_grads[3].T
    input_grad, first_shift_grad, first_gain_grad = call(
        functools.partial(input_grad_kernel, functools.partial(back_finish, total, 3, True)),
        (windows // quad,),
        [own(cot, size=quad), own(first_up[0], size=quad), own(x, size=quad)]
        + [whole(p) for p in gathered]
        + [whole(first_par)],
        [made((windows, bins, channels), size=quad), kept(channels), kept(channels)],
        [pltpu.VMEM((5, channels), F32)],
        moved=x.size * 16,
    )
    return (
        block_output,
        input_grad,
        first_gain_grad,
        first_shift_grad,
        tap_grad,
        second_gain_grad,
        second_shift_grad,
        point_grad,
    )


def solution(mesh):
    seq, dp = mesh.devices.shape
    split_mesh = Mesh(mesh.devices.reshape(seq, dp // 2, 2), ("seq",) + DP)
    rows = P(DP, "seq", None)
    return jax.shard_map(
        on_device,
        mesh=split_mesh,
        in_specs=(rows, P(), P(), P(), P(), P(), P(), rows),
        out_specs=(rows, rows, P(), P(), P(), P(), P(), P()),
        check_vma=False,
    )
```
